32 devices in a mesh: rep: 2 (over x), row: 16 (over z, y, core).
Axes of the slice: x: 2, y: 2, z: 4, core: 2. Of those that a mesh axis runs over, the one named last changes fastest.
Arguments:
- grad_out: bfloat16 [4096, 256], P(('rep', 'row')), may hold values from -6 to 6
- relu_mask: int32 [4096, 256], P(('rep', 'row')), may hold values 0 or 1
- layer_input: bfloat16 [4096, 256], P(('rep', 'row')), may hold values from -6 to 6
- weight: bfloat16 [256, 256], replicated, may hold values from -0.375 to 0.375
- tile_values: bfloat16 [4096, 128, 128], P(('rep', 'row')), may hold values from -0.0625 to 0.0625
- tile_rows: int32 [4096], P(('rep', 'row')), may hold values from 0 to 1
- tile_cols: int32 [4096], P(('rep', 'row')), may hold values from 0 to 15
- tile_count: int32 [32], P(('rep', 'row')), may hold values from 32 to 128, as said below
Outputs:
- grad_input: bfloat16 [4096, 256], P(('rep', 'row'))
- grad_weight: float32 [256, 256], replicated
The draws below stay inside these ranges and needn't reach their ends.
Inputs may be any that keep to these rules, and one draw needn't show every extreme that they name: Slots k < tile_count[d] of device d are live; some device has 128 live slots; two devices whose indices differ only in the lowest bit hold together at most 160 live slots, and some such pair reaches it.
All inputs are finite; a program needn't handle non-finite values. No bound on the sum of `relu_mask` on one device may be relied on, other than what follows from the above.
Results may differ from the reference program's by a relative error of at most 0.015.
Values may be sent and summed in bfloat16 or wider, within the bound.
No kernel may reach another device: no remote copies, remote signals or barrier semaphores. Data moves between devices by JAX's collectives and lax.ppermute only.
A program may use at most 64 MiB of HBM per device.

```python
import jax
import jax.numpy as jnp
from jax import lax

F = 256
BLK = 128
CAP = 128
NODES = 4096
SLOTS = 4096
N_REP = 2
N_ROW = 16


def draw_tile_count(key, part):
    pair_total = N_REP * N_ROW // 2
    first_key = jax.random.fold_in(key, 11)
    second_key = jax.random.fold_in(key, 12)
    order_key = jax.random.fold_in(key, 13)
    fullest_key = jax.random.fold_in(key, 14)
    first = jax.random.randint(first_key, (pair_total,), CAP // 4, CAP + 1, dtype=jnp.int32)
    spare = jax.random.randint(second_key, (pair_total,), 0, 1 << 20, dtype=jnp.int32)
    room = CAP + CAP // 4 - first - CAP // 4 + 1
    second = CAP // 4 + spare % room
    fullest = jax.random.randint(fullest_key, (), 0, pair_total, dtype=jnp.int32)
    first = first.at[fullest].set(CAP)
    second = second.at[fullest].set(CAP // 4)
    flip = jax.random.randint(order_key, (pair_total,), 0, 2, dtype=jnp.int32)
    lower = jnp.where(flip == 1, second, first)
    upper = jnp.where(flip == 1, first, second)
    return jnp.stack([lower, upper], axis=1).reshape(N_REP * N_ROW).astype(jnp.int32)


def plant(drawn, key, smallest, high):
    longest = drawn.shape.index(max(drawn.shape))
    spots = []
    for shift in (0, 1):
        where = [jax.random.randint(jax.random.fold_in(key, axis), (), 0, length) for axis, length in enumerate(drawn.shape)]
        where[longest] = (where[longest] + shift) % drawn.shape[longest]
        spots.append(tuple(where))
    return drawn.at[spots[0]].set(smallest).at[spots[1]].set(high)


def block_scale(own_key, extent, pieces, smallest, high):
    gain, own = 1.0, jax.random.fold_in(own_key, 6)
    for axis_at, parts in pieces:
        draws = jnp.exp(jax.random.uniform(jax.random.fold_in(own, axis_at), (parts,), jnp.float32, smallest / len(pieces), high / len(pieces)))
        gain = gain * jnp.repeat(draws, extent[axis_at] // parts).reshape([-1 if axis == axis_at else 1 for axis in range(len(extent))])
    return gain


def scatter_about(own_key, extent, spread, reach, split=(), kind=jnp.bfloat16):
    result = jax.random.normal(own_key, extent, jnp.float32) * spread
    if len(split) > 0:
        result = block_scale(own_key, extent, split, -0.22, 0.18) * result
    return jnp.clip(result, min=-reach, max=reach).astype(kind)


def setup_inputs(seed: int = 0) -> dict:
    splits = jax.random.split(jax.random.key(seed), 9)
    return {
        "grad_out": scatter_about(splits[0], (NODES, F), 1.0, 6.0, ((0, 32),)),
        "relu_mask": plant((jax.random.randint(splits[1], (NODES, F), 0, 2) < 1).astype(jnp.int32), jax.random.fold_in(splits[1], 1), 0, 1),
        "layer_input": scatter_about(splits[2], (NODES, F), 1.0, 6.0, ((0, 32),)),
        "weight": scatter_about(splits[3], (F, F), F ** -0.5, 0.375),
        "tile_values": scatter_about(splits[4], (SLOTS, BLK, BLK), (BLK * CAP // N_REP) ** -0.5, 0.0625, ((0, 32),)),
        "tile_rows": plant(jax.random.randint(splits[5], (SLOTS,), 0, N_REP), jax.random.fold_in(splits[5], 1), 0, N_REP - 1).astype(jnp.int32),
        "tile_cols": plant(jax.random.randint(splits[6], (SLOTS,), 0, N_ROW), jax.random.fold_in(splits[6], 1), 0, N_ROW - 1).astype(jnp.int32),
        "tile_count": draw_tile_count(jax.random.fold_in(splits[8], 71), 0),
    }


def reference(grad_out, relu_mask, layer_input, weight, tile_values, tile_rows, tile_cols, tile_count):
    features = grad_out.shape[1]
    masked = grad_out * relu_mask.astype(jnp.bfloat16)
    node_blocks = masked.reshape(N_REP * N_ROW, BLK, features)
    all_values = tile_values.reshape(N_REP * N_ROW, CAP, BLK, BLK)
    all_rows = tile_rows.reshape(N_REP * N_ROW, CAP)
    all_cols = tile_cols.reshape(N_REP * N_ROW, CAP)

    def device_step(totals, device_id):
        rep_id = device_id // N_ROW
        row_id = device_id % N_ROW
        in_blocks = (rep_id * N_ROW + all_cols[device_id]).astype(jnp.int32)
        out_blocks = (all_rows[device_id] * N_ROW + row_id).astype(jnp.int32)
        sources = node_blocks[in_blocks].astype(jnp.float32)
        products = jnp.einsum("kab,kbf->kaf", all_values[device_id].astype(jnp.float32), sources)
        alive_mask = (jnp.arange(CAP, dtype=jnp.int32) < tile_count[device_id]).astype(jnp.float32)
        products = products * alive_mask[:, None, None]
        return totals.at[out_blocks].add(products), None

    start_totals = jnp.zeros((N_REP * N_ROW, BLK, features), jnp.float32)
    prop_grad, _ = lax.scan(device_step, start_totals, jnp.arange(N_REP * N_ROW, dtype=jnp.int32))
    prop_rounded = prop_grad.reshape(-1, features).astype(jnp.bfloat16)
    grad_input = jnp.dot(prop_rounded, weight.T, preferred_element_type=jnp.float32).astype(jnp.bfloat16)
    grad_weight = jnp.dot(layer_input.T, prop_rounded, preferred_element_type=jnp.float32)
    grad_weight = grad_weight * (1.0 / (NODES ** 0.5))
    return grad_input, grad_weight
```

```python
import functools

import jax
import jax.numpy as jnp
from jax import lax
from jax.experimental import pallas as pl
from jax.experimental.pallas import tpu as pltpu
from jax.sharding import PartitionSpec as P

slot_group = 8
both = ("rep", "row")


def tile_pass(values, rows_ids, cols_ids, live_count, sources, out_blocks):
    block_rows = values.shape[1]
    features = sources.shape[2]
    slot_total = values.shape[0]

    def one_turn(turn_id, totals):
        slot_ids = turn_id * slot_group + jnp.arange(slot_group, dtype=jnp.int32)
        alive_mask = slot_ids < live_count
        clipped = jnp.minimum(slot_ids, slot_total - 1)
        tile_block = values[clipped]
        picked = sources[cols_ids[clipped]]
        products = jnp.einsum(
            "kab,kbf->kaf", tile_block, picked, preferred_element_type=jnp.float32
        )
        onehot = (
            rows_ids[clipped][None, :] == jnp.arange(out_blocks, dtype=jnp.int32)[:, None]
        ) & alive_mask[None, :]
        return totals + jnp.einsum("rk,kaf->raf", onehot.astype(jnp.float32), products)

    turn_count = (live_count + slot_group - 1) // slot_group
    start_totals = jnp.zeros((out_blocks, block_rows, features), jnp.float32)
    return lax.fori_loop(0, turn_count, one_turn, start_totals)


def general_body(grad_out, relu_mask, layer_input, weight, tile_values, tile_rows, tile_cols, tile_count):
    block_rows = tile_values.shape[1]
    features = grad_out.shape[1]
    out_blocks = lax.axis_size("rep")
    nodes_total = block_rows * lax.axis_size("rep") * lax.axis_size("row")
    masked = grad_out * relu_mask.astype(jnp.bfloat16)
    group_rows = lax.all_gather(masked, "row", axis=0, tiled=True)
    sources = group_rows.reshape(-1, block_rows, features)
    live_count = tile_count[0]
    partial_value = tile_pass(tile_values, tile_rows, tile_cols, live_count, sources, out_blocks)
    partial_value = partial_value.reshape(out_blocks * block_rows, features)
    owned = lax.psum_scatter(partial_value, "rep", scatter_dimension=0, tiled=True)
    prop_rounded = owned.astype(jnp.bfloat16)
    grad_input = lax.dot_general(
        prop_rounded, weight, (((1,), (1,)), ((), ())), preferred_element_type=jnp.float32
    ).astype(jnp.bfloat16)
    local_terms = lax.dot_general(
        layer_input, prop_rounded, (((0,), (0,)), ((), ())), preferred_element_type=jnp.float32
    )
    grad_weight = lax.psum(local_terms, both) * (1.0 / nodes_total**0.5)
    return (grad_input, grad_weight)


def swap(value, mask, total):
    return lax.ppermute(value, both, [(i, i ^ mask) for i in range(total)])


def merge_kernel(order, group, place_ref, rows_ref, cols_ref, count_ref, values_ref, out_ref, staged, sums, sems):
    slots = values_ref.shape[0]
    sources = len(order)
    blk = values_ref.shape[1]
    count = count_ref[0]
    pieces = slots // group

    def piece_copy(i):
        part = pl.ds(i * group, group)
        return pltpu.make_async_copy(values_ref.at[part], staged.at[part], sems.at[i])

    for i in range(pieces):
        @pl.when(i * group < count)
        def _(i=i):
            piece_copy(i).start()

    sums[...] = jnp.zeros_like(sums)
    rep_id = place_ref[0]
    row_id = place_ref[1]
    for i in range(pieces):
        @pl.when(i * group < count)
        def _(i=i):
            piece_copy(i).wait()

            def add_one(k, carry):
                spot = (rows_ref[k] ^ rep_id) * sources + (cols_ref[k] ^ row_id)
                sums[spot] += staged[k].astype(jnp.float32)
                return carry

            lax.fori_loop(i * group, jnp.minimum(count, (i + 1) * group), add_one, 0)

    for r in range(out_ref.shape[0] // blk):
        for at, offset in enumerate(order):
            out_ref[r * blk:(r + 1) * blk, at * blk:(at + 1) * blk] = sums[r * sources + offset].astype(out_ref.dtype)


def merge_tiles(place, rows, cols, count, values, order, out_blocks):
    slots, blk, _ = values.shape
    group = 16
    smem = pl.BlockSpec(memory_space=pltpu.SMEM)
    return pl.pallas_call(
        functools.partial(merge_kernel, order, group),
        out_shape=jax.ShapeDtypeStruct((out_blocks * blk, len(order) * blk), jnp.bfloat16),
        in_specs=[smem, smem, smem, smem, pl.BlockSpec(memory_space=pl.ANY)],
        out_specs=pl.BlockSpec(memory_space=pltpu.VMEM),
        scratch_shapes=[
            pltpu.VMEM(values.shape, values.dtype),
            pltpu.VMEM((out_blocks * len(order), blk, blk), jnp.float32),
            pltpu.SemaphoreType.DMA((slots // group,)),
        ],
        compiler_params=pltpu.CompilerParams(vmem_limit_bytes=24 * 1024 * 1024),
        cost_estimate=pl.CostEstimate(flops=slots * blk * blk, bytes_accessed=4 * slots * blk * blk, transcendentals=0),
    )(place, rows, cols, count, values)


def product_kernel(scale, place_ref, tiles_ref, near_ref, far_ref, own_in_ref, peer_in_ref, keep_ref, send_ref, own_ref, peer_ref):
    half = near_ref.shape[0]
    blk = own_in_ref.shape[0]
    total = jnp.dot(tiles_ref[:, :half], near_ref[...], preferred_element_type=jnp.float32)
    total += jnp.dot(tiles_ref[:, half:], far_ref[...], preferred_element_type=jnp.float32)
    own_ref[...] = total[:blk]
    peer_ref[...] = total[blk:].astype(peer_ref.dtype)
    rounded = total.astype(jnp.bfloat16)
    across = (((0,), (0,)), ((), ()))
    terms = lax.dot_general(own_in_ref[...], rounded[:blk], across, preferred_element_type=jnp.float32)
    terms += lax.dot_general(peer_in_ref[...], rounded[blk:], across, preferred_element_type=jnp.float32)
    terms *= scale
    rows = terms.shape[0] // 2
    upper = place_ref[2] == 0
    keep_ref[...] = jnp.where(upper, terms[:rows], terms[rows:])
    send_ref[...] = jnp.where(upper, terms[rows:], terms[:rows])


def products(place, tiles, near, far, own_in, peer_in, scale):
    blk, features = own_in.shape
    vmem = pl.BlockSpec(memory_space=pltpu.VMEM)
    part = (own_in.shape[1] // 2, features)
    return pl.pallas_call(
        functools.partial(product_kernel, scale),
        out_shape=[
            jax.ShapeDtypeStruct(part, jnp.float32),
            jax.ShapeDtypeStruct(part, jnp.float32),
            jax.ShapeDtypeStruct((blk, features), jnp.float32),
            jax.ShapeDtypeStruct((blk, features), jnp.bfloat16),
        ],
        in_specs=[pl.BlockSpec(memory_space=pltpu.SMEM)] + [vmem] * 5,
        out_specs=[vmem] * 4,
        compiler_params=pltpu.CompilerParams(vmem_limit_bytes=24 * 1024 * 1024),
        cost_estimate=pl.CostEstimate(flops=2 * tiles.size * features, bytes_accessed=4 * tiles.size, transcendentals=0),
    )(place, tiles, near, far, own_in, peer_in)


def quad_sum(value, low, high, total):
    first = swap(value, low, total)
    second = swap(value, high, total)
    third = swap(value, low | high, total)
    f32 = jnp.float32
    return (value.astype(f32) + first.astype(f32)) + (second.astype(f32) + third.astype(f32))


def pair_body(grad_out, relu_mask, layer_input, weight, tile_values, tile_rows, tile_cols, tile_count):
    rep, row = lax.axis_size("rep"), lax.axis_size("row")
    total = rep * row
    blk = tile_values.shape[1]
    masked = grad_out * relu_mask.astype(jnp.bfloat16)
    rep_id, row_id = lax.axis_index("rep"), lax.axis_index("row")
    core_id = row_id % 2
    place = jnp.stack([rep_id, row_id, core_id]).astype(jnp.int32)

    order = [0]
    gathered = [masked]
    top = row // 4
    gathered = [masked] + [swap(masked, m, total) for m in (top, 2 * top, 3 * top)]
    order = [0, top, 2 * top, 3 * top]
    near = jnp.concatenate(gathered, 0)
    bit = top // 2
    while bit > 1:
        near = jnp.concatenate([near, swap(near, bit, total)], 0)
        order = order + [o ^ bit for o in order]
        bit //= 2
    far = swap(near, 1, total)
    order = order + [o ^ 1 for o in order]
    peer_in = swap(layer_input, row, total)
    tiles = merge_tiles(place, tile_rows, tile_cols, tile_count, tile_values, order, rep)
    keep, send, own, peer = products(place, tiles, near, far, layer_input, peer_in, 1.0 / (blk * total) ** 0.5)

    part = (keep + swap(send, 1, total)).astype(jnp.bfloat16)
    part = lax.optimization_barrier(part)
    part = quad_sum(part, row, top // 2, total).astype(jnp.bfloat16)
    part = lax.optimization_barrier(part)
    part = quad_sum(part, top, 2 * top, total)
    part = lax.optimization_barrier(part)
    other = swap(part, 1, total)
    grad_weight = jnp.where(core_id == 0, jnp.concatenate([part, other], 0), jnp.concatenate([other, part], 0))

    prop = (own + swap(peer, row, total).astype(jnp.float32)).astype(jnp.bfloat16)
    grad_input = lax.dot_general(
        prop, weight, (((1,), (1,)), ((), ())), preferred_element_type=jnp.float32
    ).astype(jnp.bfloat16)
    return (grad_input, grad_weight)


def solution(mesh):
    placed = (
        P(both, None),
        P(both, None),
        P(both, None),
        P(),
        P(both, None, None),
        P(both),
        P(both),
        P(both),
    )
    merged = mesh.shape["rep"] == 2 and mesh.shape["row"] == 16
    return jax.shard_map(
        pair_body if merged else general_body,
        mesh=mesh,
        in_specs=placed,
        out_specs=(P(both, None), P()),
        check_vma=False,
    )
```

```python
import functools

import jax
import jax.numpy as jnp
from jax import lax
from jax.experimental import pallas as pl
from jax.experimental.pallas import tpu as pltpu
from jax.sharding import PartitionSpec as P

slot_group = 8
both = ("rep", "row")


def tile_pass(values, rows_ids, cols_ids, live_count, sources, out_blocks):
    block_rows = values.shape[1]
    features = sources.shape[2]
    slot_total = values.shape[0]

    def one_turn(turn_id, totals):
        slot_ids = turn_id * slot_group + jnp.arange(slot_group, dtype=jnp.int32)
        alive_mask = slot_ids < live_count
        clipped = jnp.minimum(slot_ids, slot_total - 1)
        tile_block = values[clipped]
        picked = sources[cols_ids[clipped]]
        products = jnp.einsum(
            "kab,kbf->kaf", tile_block, picked, preferred_element_type=jnp.float32
        )
        onehot = (
            rows_ids[clipped][None, :] == jnp.arange(out_blocks, dtype=jnp.int32)[:, None]
        ) & alive_mask[None, :]
        return totals + jnp.einsum("rk,kaf->raf", onehot.astype(jnp.float32), products)

    turn_count = (live_count + slot_group - 1) // slot_group
    start_totals = jnp.zeros((out_blocks, block_rows, features), jnp.float32)
    return lax.fori_loop(0, turn_count, one_turn, start_totals)


def general_body(grad_out, relu_mask, layer_input, weight, tile_values, tile_rows, tile_cols, tile_count):
    block_rows = tile_values.shape[1]
    features = grad_out.shape[1]
    out_blocks = lax.axis_size("rep")
    nodes_total = block_rows * lax.axis_size("rep") * lax.axis_size("row")
    masked = grad_out * relu_mask.astype(jnp.bfloat16)
    group_rows = lax.all_gather(masked, "row", axis=0, tiled=True)
    sources = group_rows.reshape(-1, block_rows, features)
    live_count = tile_count[0]
    partial_value = tile_pass(tile_values, tile_rows, tile_cols, live_count, sources, out_blocks)
    partial_value = partial_value.reshape(out_blocks * block_rows, features)
    owned = lax.psum_scatter(partial_value, "rep", scatter_dimension=0, tiled=True)
    prop_rounded = owned.astype(jnp.bfloat16)
    grad_input = lax.dot_general(
        prop_rounded, weight, (((1,), (1,)), ((), ())), preferred_element_type=jnp.float32
    ).astype(jnp.bfloat16)
    local_terms = lax.dot_general(
        layer_input, prop_rounded, (((0,), (0,)), ((), ())), preferred_element_type=jnp.float32
    )
    grad_weight = lax.psum(local_terms, both) * (1.0 / nodes_total**0.5)
    return (grad_input, grad_weight)


def swap(value, mask, total):
    return lax.ppermute(value, both, [(i, i ^ mask) for i in range(total)])


def merge_kernel(order, group, spots_ref, values_ref, *rest):
    halves, (staged, sems), sums = rest[:2], rest[2:4], rest[4:]
    slots = values_ref.shape[0]
    sources = len(order)
    blk = values_ref.shape[1]
    count = spots_ref[slots]
    pieces = slots // group
    ways = len(sums)
    spare = sums[0].shape[0] - 1

    def piece_copy(i):
        part = pl.ds(i * group, group)
        return pltpu.make_async_copy(values_ref.at[part], staged.at[part], sems.at[i])

    for i in range(pieces):
        @pl.when(i * group < count)
        def _(i=i):
            piece_copy(i).start()

    for total in sums:
        total[...] = jnp.zeros_like(total)
    for i in range(pieces):
        @pl.when(i * group < count)
        def _(i=i):
            piece_copy(i).wait()

            def add_some(turn, carry):
                for way, total in enumerate(sums):
                    k = turn * ways + way
                    spot = jnp.where(k < count, spots_ref[k], spare)
                    total[spot] += staged[k].astype(jnp.float32)
                return carry

            last = jnp.minimum(count, (i + 1) * group)
            lax.fori_loop(i * group // ways, (last + ways - 1) // ways, add_some, 0)

    for h, half in enumerate(halves):
        across = half.shape[1] // blk
        for r in range(half.shape[0] // blk):
            for at in range(across):
                spot = r * sources + order[h * across + at]
                half[r * blk:(r + 1) * blk, at * blk:(at + 1) * blk] = sum(total[spot] for total in sums).astype(half.dtype)


def merge_tiles(spots, values, order, out_blocks):
    slots, blk, _ = values.shape
    group, ways = 16, 2
    smem = pl.BlockSpec(memory_space=pltpu.SMEM)
    vmem = pl.BlockSpec(memory_space=pltpu.VMEM)
    half = jax.ShapeDtypeStruct((out_blocks * blk, len(order) // 2 * blk), jnp.bfloat16)
    return pl.pallas_call(
        functools.partial(merge_kernel, order, group),
        out_shape=[half, half],
        in_specs=[smem, pl.BlockSpec(memory_space=pltpu.HBM)],
        out_specs=[vmem, vmem],
        scratch_shapes=[
            pltpu.VMEM(values.shape, values.dtype),
            pltpu.SemaphoreType.DMA((slots // group,)),
        ] + [pltpu.VMEM((out_blocks * len(order) + 1, blk, blk), jnp.float32)] * ways,
        compiler_params=pltpu.CompilerParams(vmem_limit_bytes=50 * 1024 * 1024),
        cost_estimate=pl.CostEstimate(flops=slots * blk * blk, bytes_accessed=4 * slots * blk * blk, transcendentals=0),
    )(spots, values)


def product_kernel(scale, place_ref, own_tiles_ref, twin_tiles_ref, near_ref, own_in_ref, twin_in_ref, keep_ref, send_ref, own_ref, twin_ref):
    own = jnp.dot(own_tiles_ref[...], near_ref[...], preferred_element_type=jnp.float32)
    twin = jnp.dot(twin_tiles_ref[...], near_ref[...], preferred_element_type=jnp.float32)
    own_ref[...] = own
    twin_ref[...] = twin.astype(twin_ref.dtype)
    across = (((0,), (0,)), ((), ()))
    terms = lax.dot_general(own_in_ref[...], own.astype(jnp.bfloat16), across, preferred_element_type=jnp.float32)
    terms += lax.dot_general(twin_in_ref[...], twin.astype(jnp.bfloat16), across, preferred_element_type=jnp.float32)
    terms *= scale
    rows = terms.shape[0] // 2
    upper = place_ref[0] == 0
    keep_ref[...] = jnp.where(upper, terms[:rows], terms[rows:])
    send_ref[...] = jnp.where(upper, terms[rows:], terms[:rows])


def products(place, own_tiles, twin_tiles, near, own_in, twin_in, scale):
    rows, features = own_tiles.shape[0], near.shape[1]
    vmem = pl.BlockSpec(memory_space=pltpu.VMEM)
    part = (own_in.shape[1] // 2, features)
    return pl.pallas_call(
        functools.partial(product_kernel, scale),
        out_shape=[
            jax.ShapeDtypeStruct(part, jnp.float32),
            jax.ShapeDtypeStruct(part, jnp.float32),
            jax.ShapeDtypeStruct((rows, features), jnp.float32),
            jax.ShapeDtypeStruct((rows, features), jnp.bfloat16),
        ],
        in_specs=[pl.BlockSpec(memory_space=pltpu.SMEM)] + [vmem] * 5,
        out_specs=[vmem] * 4,
        compiler_params=pltpu.CompilerParams(vmem_limit_bytes=24 * 1024 * 1024),
        cost_estimate=pl.CostEstimate(flops=4 * own_tiles.size * features, bytes_accessed=4 * own_tiles.size, transcendentals=0),
    )(place, own_tiles, twin_tiles, near, own_in, twin_in)


def quad_sum(value, low, high, total):
    third = swap(value, low | high, total)
    second = swap(value, high, total)
    first = swap(value, low, total)
    f32 = jnp.float32
    return (third.astype(f32) + second.astype(f32)) + (first.astype(f32) + value.astype(f32))


def pair_body(grad_out, relu_mask, layer_input, weight, tile_values, tile_rows, tile_cols, tile_count):
    rep, row = lax.axis_size("rep"), lax.axis_size("row")
    total = rep * row
    blk = tile_values.shape[1]
    masked = grad_out * relu_mask.astype(jnp.bfloat16)
    rep_id, row_id = lax.axis_index("rep"), lax.axis_index("row")
    core_id = row_id % 2
    place = core_id.astype(jnp.int32).reshape(1)

    top = row // 4
    order = [0, 3 * top, 2 * top, top]
    near = jnp.concatenate([masked] + [swap(masked, m, total) for m in order[1:]], 0)
    spots = (tile_rows ^ rep_id) * row + (tile_cols ^ row_id)
    spots = jnp.concatenate([spots, tile_count])
    order = order + [o + 2 for o in order]
    order = order + [o + 1 for o in order]
    own_tiles, far_tiles = merge_tiles(spots, tile_values, order, rep)
    near, own_tiles, far_tiles, own_in = lax.optimization_barrier((near, own_tiles, far_tiles, layer_input))
    near = jnp.concatenate([near, swap(near, 2, total)], 0)
    own_in = jnp.concatenate([own_in, swap(own_in, row, total)], 0)
    twin_tiles = swap(far_tiles, 1, total)
    own_in, twin_tiles = lax.optimization_barrier((own_in, twin_tiles))
    twin_in = swap(own_in, 1, total)
    near, own_in, twin_in, twin_tiles = lax.optimization_barrier((near, own_in, twin_in, twin_tiles))
    keep, send, own, twin = products(place, own_tiles, twin_tiles, near, own_in, twin_in, 1.0 / (blk * total) ** 0.5)

    part = (keep + swap(send, 1, total)).astype(jnp.bfloat16)
    part = lax.optimization_barrier(part)
    part = quad_sum(part, row, top // 2, total).astype(jnp.bfloat16)
    part = lax.optimization_barrier(part)
    part = quad_sum(part, top, 2 * top, total)
    part = lax.optimization_barrier(part)
    other = swap(part, 1, total)
    grad_weight = jnp.where(core_id == 0, jnp.concatenate([part, other], 0), jnp.concatenate([other, part], 0))

    own = own + swap(twin, 1, total).astype(jnp.float32)
    peer = swap(own[blk:].astype(jnp.bfloat16), row, total)
    prop = (own[:blk] + peer.astype(jnp.float32)).astype(jnp.bfloat16)
    grad_input = lax.dot_general(
        prop, weight, (((1,), (1,)), ((), ())), preferred_element_type=jnp.float32
    ).astype(jnp.bfloat16)
    return (grad_input, grad_weight)


def solution(mesh):
    placed = (
        P(both, None),
        P(both, None),
        P(both, None),
        P(),
        P(both, None, None),
        P(both),
        P(both),
        P(both),
    )
    merged = mesh.shape["rep"] == 2 and mesh.shape["row"] == 16
    return jax.shard_map(
        pair_body if merged else general_body,
        mesh=mesh,
        in_specs=placed,
        out_specs=(P(both, None), P()),
        check_vma=False,
    )
```

```python
import functools

import jax
import jax.numpy as jnp
from jax import lax
from jax.experimental import pallas as pl
from jax.experimental.pallas import tpu as pltpu
from jax.sharding import PartitionSpec as P

slot_group = 8
both = ("rep", "row")


def tile_pass(values, rows_ids, cols_ids, live_count, sources, out_blocks):
    block_rows = values.shape[1]
    features = sources.shape[2]
    slot_total = values.shape[0]

    def one_turn(turn_id, totals):
        slot_ids = turn_id * slot_group + jnp.arange(slot_group, dtype=jnp.int32)
        alive_mask = slot_ids < live_count
        clipped = jnp.minimum(slot_ids, slot_total - 1)
        tile_block = values[clipped]
        picked = sources[cols_ids[clipped]]
        products = jnp.einsum(
            "kab,kbf->kaf", tile_block, picked, preferred_element_type=jnp.float32
        )
        onehot = (
            rows_ids[clipped][None, :] == jnp.arange(out_blocks, dtype=jnp.int32)[:, None]
        ) & alive_mask[None, :]
        return totals + jnp.einsum("rk,kaf->raf", onehot.astype(jnp.float32), products)

    turn_count = (live_count + slot_group - 1) // slot_group
    start_totals = jnp.zeros((out_blocks, block_rows, features), jnp.float32)
    return lax.fori_loop(0, turn_count, one_turn, start_totals)


def general_body(grad_out, relu_mask, layer_input, weight, tile_values, tile_rows, tile_cols, tile_count):
    block_rows = tile_values.shape[1]
    features = grad_out.shape[1]
    out_blocks = lax.axis_size("rep")
    nodes_total = block_rows * lax.axis_size("rep") * lax.axis_size("row")
    masked = grad_out * relu_mask.astype(jnp.bfloat16)
    group_rows = lax.all_gather(masked, "row", axis=0, tiled=True)
    sources = group_rows.reshape(-1, block_rows, features)
    live_count = tile_count[0]
    partial_value = tile_pass(tile_values, tile_rows, tile_cols, live_count, sources, out_blocks)
    partial_value = partial_value.reshape(out_blocks * block_rows, features)
    owned = lax.psum_scatter(partial_value, "rep", scatter_dimension=0, tiled=True)
    prop_rounded = owned.astype(jnp.bfloat16)
    grad_input = lax.dot_general(
        prop_rounded, weight, (((1,), (1,)), ((), ())), preferred_element_type=jnp.float32
    ).astype(jnp.bfloat16)
    local_terms = lax.dot_general(
        layer_input, prop_rounded, (((0,), (0,)), ((), ())), preferred_element_type=jnp.float32
    )
    grad_weight = lax.psum(local_terms, both) * (1.0 / nodes_total**0.5)
    return (grad_input, grad_weight)


def swap(value, mask, total):
    return lax.ppermute(value, both, [(i, i ^ mask) for i in range(total)])


def merge_kernel(order, group, spots_ref, values_ref, *rest):
    halves, (staged, sems), sums = rest[:2], rest[2:4], rest[4:]
    slots = values_ref.shape[0]
    sources = len(order)
    blk = values_ref.shape[1]
    count = spots_ref[slots]
    pieces = slots // group
    ways = len(sums)
    spare = sums[0].shape[0] - 1

    def piece_copy(i):
        part = pl.ds(i * group, group)
        return pltpu.make_async_copy(values_ref.at[part], staged.at[part], sems.at[i])

    for i in range(pieces):
        @pl.when(i * group < count)
        def _(i=i):
            piece_copy(i).start()

    for total in sums:
        total[...] = jnp.zeros_like(total)
    for i in range(pieces):
        @pl.when(i * group < count)
        def _(i=i):
            piece_copy(i).wait()

            def add_some(turn, carry):
                for way, total in enumerate(sums):
                    k = turn * ways + way
                    spot = jnp.where(k < count, spots_ref[k], spare)
                    total[spot] += staged[k].astype(jnp.float32)
                return carry

            last = jnp.minimum(count, (i + 1) * group)
            lax.fori_loop(i * group // ways, (last + ways - 1) // ways, add_some, 0)

    for h, half in enumerate(halves):
        across = half.shape[1] // blk
        for r in range(half.shape[0] // blk):
            for at in range(across):
                spot = r * sources + order[h * across + at]
                half[r * blk:(r + 1) * blk, at * blk:(at + 1) * blk] = sum(total[spot] for total in sums).astype(half.dtype)


def merge_tiles(spots, values, order, out_blocks):
    slots, blk, _ = values.shape
    group, ways = 16, 2
    smem = pl.BlockSpec(memory_space=pltpu.SMEM)
    vmem = pl.BlockSpec(memory_space=pltpu.VMEM)
    half = jax.ShapeDtypeStruct((out_blocks * blk, len(order) // 2 * blk), jnp.bfloat16)
    return pl.pallas_call(
        functools.partial(merge_kernel, order, group),
        out_shape=[half, half],
        in_specs=[smem, pl.BlockSpec(memory_space=pltpu.HBM)],
        out_specs=[vmem, vmem],
        scratch_shapes=[
            pltpu.VMEM(values.shape, values.dtype),
            pltpu.SemaphoreType.DMA((slots // group,)),
        ] + [pltpu.VMEM((out_blocks * len(order) + 1, blk, blk), jnp.float32)] * ways,
        compiler_params=pltpu.CompilerParams(vmem_limit_bytes=50 * 1024 * 1024),
        cost_estimate=pl.CostEstimate(flops=slots * blk * blk, bytes_accessed=4 * slots * blk * blk, transcendentals=0),
    )(spots, values)


def product_kernel(scale, place_ref, own_tiles_ref, twin_tiles_ref, near_ref, own_in_ref, twin_in_ref, keep_ref, send_ref, own_ref, twin_ref):
    own = jnp.dot(own_tiles_ref[...], near_ref[...], preferred_element_type=jnp.float32)
    twin = jnp.dot(twin_tiles_ref[...], near_ref[...], preferred_element_type=jnp.float32)
    own_ref[...] = own
    twin_ref[...] = twin.astype(twin_ref.dtype)
    across = (((0,), (0,)), ((), ()))
    terms = lax.dot_general(own_in_ref[...], own.astype(jnp.bfloat16), across, preferred_element_type=jnp.float32)
    terms += lax.dot_general(twin_in_ref[...], twin.astype(jnp.bfloat16), across, preferred_element_type=jnp.float32)
    terms *= scale
    rows = terms.shape[0] // 2
    upper = place_ref[0] == 0
    keep_ref[...] = jnp.where(upper, terms[:rows], terms[rows:])
    send_ref[...] = jnp.where(upper, terms[rows:], terms[:rows])


def products(place, own_tiles, twin_tiles, near, own_in, twin_in, scale):
    rows, features = own_tiles.shape[0], near.shape[1]
    vmem = pl.BlockSpec(memory_space=pltpu.VMEM)
    part = (own_in.shape[1] // 2, features)
    return pl.pallas_call(
        functools.partial(product_kernel, scale),
        out_shape=[
            jax.ShapeDtypeStruct(part, jnp.float32),
            jax.ShapeDtypeStruct(part, jnp.float32),
            jax.ShapeDtypeStruct((rows, features), jnp.float32),
            jax.ShapeDtypeStruct((rows, features), jnp.bfloat16),
        ],
        in_specs=[pl.BlockSpec(memory_space=pltpu.SMEM)] + [vmem] * 5,
        out_specs=[vmem] * 4,
        compiler_params=pltpu.CompilerParams(vmem_limit_bytes=24 * 1024 * 1024),
        cost_estimate=pl.CostEstimate(flops=4 * own_tiles.size * features, bytes_accessed=4 * own_tiles.size, transcendentals=0),
    )(place, own_tiles, twin_tiles, near, own_in, twin_in)


def core_swap(value, masks, total):
    return lax.ppermute(value, both, [(i, i ^ masks[i % 2]) for i in range(total)])


def quad_sum(value, low, high, total):
    third = core_swap(value, [a | b for a, b in zip(low, high)], total)
    second = core_swap(value, high, total)
    first = core_swap(value, low, total)
    f32 = jnp.float32
    return (third.astype(f32) + second.astype(f32)) + (first.astype(f32) + value.astype(f32))


def pair_body(grad_out, relu_mask, layer_input, weight, tile_values, tile_rows, tile_cols, tile_count):
    rep, row = lax.axis_size("rep"), lax.axis_size("row")
    total = rep * row
    blk = tile_values.shape[1]
    masked = grad_out * relu_mask.astype(jnp.bfloat16)
    rep_id, row_id = lax.axis_index("rep"), lax.axis_index("row")
    core_id = row_id % 2
    place = core_id.astype(jnp.int32).reshape(1)

    top = row // 4
    order = [0, 3 * top, 2 * top, top]
    near = jnp.concatenate([masked] + [swap(masked, m, total) for m in order[1:]], 0)
    spots = (tile_rows ^ rep_id) * row + (tile_cols ^ row_id)
    spots = jnp.concatenate([spots, tile_count])
    order = order + [o + 2 for o in order]
    order = order + [o + 1 for o in order]
    other_in = swap(layer_input, row, total)
    own_tiles, far_tiles = merge_tiles(spots, tile_values, order, rep)
    other_in, own_tiles, far_tiles, near = lax.optimization_barrier((other_in, own_tiles, far_tiles, near))
    near = jnp.concatenate([near, swap(near, 2, total)], 0)
    own_in = jnp.concatenate([layer_input, other_in], 0)
    rows = far_tiles.shape[0] // 2
    twin_tiles = jnp.concatenate([swap(far_tiles[i * rows:(i + 1) * rows], 1, total) for i in range(2)], 0)
    twin_in = swap(own_in, 1, total)
    near, own_in, twin_in, twin_tiles = lax.optimization_barrier((near, own_in, twin_in, twin_tiles))
    keep, send, own, twin = products(place, own_tiles, twin_tiles, near, own_in, twin_in, 1.0 / (blk * total) ** 0.5)

    part = (keep + swap(send, 1, total)).astype(jnp.bfloat16)
    part = lax.optimization_barrier(part)
    part = quad_sum(part, (top, row), (2 * top, top // 2), total).astype(jnp.bfloat16)
    part = lax.optimization_barrier(part)
    part = quad_sum(part, (row, top), (top // 2, 2 * top), total)
    part = lax.optimization_barrier(part)
    other = swap(part, 1, total)
    grad_weight = jnp.where(core_id == 0, jnp.concatenate([part, other], 0), jnp.concatenate([other, part], 0))

    cross = jnp.concatenate([own[blk:].astype(jnp.bfloat16), twin[blk:]], 0)
    cross = swap(cross, row, total).astype(jnp.float32)
    twin = (twin[:blk].astype(jnp.float32) + cross[blk:]).astype(jnp.bfloat16)
    prop = (own[:blk] + cross[:blk] + swap(twin, 1, total).astype(jnp.float32)).astype(jnp.bfloat16)
    grad_input = lax.dot_general(
        prop, weight, (((1,), (1,)), ((), ())), preferred_element_type=jnp.float32
    ).astype(jnp.bfloat16)
    return (grad_input, grad_weight)


def solution(mesh):
    placed = (
        P(both, None),
        P(both, None),
        P(both, None),
        P(),
        P(both, None, None),
        P(both),
        P(both),
        P(both),
    )
    merged = mesh.shape["rep"] == 2 and mesh.shape["row"] == 16
    return jax.shard_map(
        pair_body if merged else general_body,
        mesh=mesh,
        in_specs=placed,
        out_specs=(P(both, None), P()),
        check_vma=False,
    )
```

```python
import functools

import jax
import jax.numpy as jnp
from jax import lax
from jax.experimental import pallas as pl
from jax.experimental.pallas import tpu as pltpu
from jax.sharding import PartitionSpec as P

slot_group = 8
both = ("rep", "row")


def tile_pass(values, rows_ids, cols_ids, live_count, sources, out_blocks):
    block_rows = values.shape[1]
    features = sources.shape[2]
    slot_total = values.shape[0]

    def one_turn(turn_id, totals):
        slot_ids = turn_id * slot_group + jnp.arange(slot_group, dtype=jnp.int32)
        alive_mask = slot_ids < live_count
        clipped = jnp.minimum(slot_ids, slot_total - 1)
        tile_block = values[clipped]
        picked = sources[cols_ids[clipped]]
        products = jnp.einsum(
            "kab,kbf->kaf", tile_block, picked, preferred_element_type=jnp.float32
        )
        onehot = (
            rows_ids[clipped][None, :] == jnp.arange(out_blocks, dtype=jnp.int32)[:, None]
        ) & alive_mask[None, :]
        return totals + jnp.einsum("rk,kaf->raf", onehot.astype(jnp.float32), products)

    turn_count = (live_count + slot_group - 1) // slot_group
    start_totals = jnp.zeros((out_blocks, block_rows, features), jnp.float32)
    return lax.fori_loop(0, turn_count, one_turn, start_totals)


def general_body(grad_out, relu_mask, layer_input, weight, tile_values, tile_rows, tile_cols, tile_count):
    block_rows = tile_values.shape[1]
    features = grad_out.shape[1]
    out_blocks = lax.axis_size("rep")
    nodes_total = block_rows * lax.axis_size("rep") * lax.axis_size("row")
    masked = grad_out * relu_mask.astype(jnp.bfloat16)
    group_rows = lax.all_gather(masked, "row", axis=0, tiled=True)
    sources = group_rows.reshape(-1, block_rows, features)
    live_count = tile_count[0]
    partial_value = tile_pass(tile_values, tile_rows, tile_cols, live_count, sources, out_blocks)
    partial_value = partial_value.reshape(out_blocks * block_rows, features)
    owned = lax.psum_scatter(partial_value, "rep", scatter_dimension=0, tiled=True)
    prop_rounded = owned.astype(jnp.bfloat16)
    grad_input = lax.dot_general(
        prop_rounded, weight, (((1,), (1,)), ((), ())), preferred_element_type=jnp.float32
    ).astype(jnp.bfloat16)
    local_terms = lax.dot_general(
        layer_input, prop_rounded, (((0,), (0,)), ((), ())), preferred_element_type=jnp.float32
    )
    grad_weight = lax.psum(local_terms, both) * (1.0 / nodes_total**0.5)
    return (grad_input, grad_weight)


def swap(value, mask, total):
    return lax.ppermute(value, both, [(i, i ^ mask) for i in range(total)])


def merge_kernel(order, group, spots_in_ref, values_ref, *rest):
    halves, (staged, spots_ref, sems, spots_sem), sums = rest[:2], rest[2:6], rest[6:]
    slots = values_ref.shape[0]
    sources = len(order)
    blk = values_ref.shape[1]
    pieces = slots // group
    ways = len(sums)
    spare = sums[0].shape[0] - 1

    def piece_copy(i):
        part = pl.ds(i * group, group)
        return pltpu.make_async_copy(values_ref.at[part], staged.at[part], sems.at[i])

    spots_copy = pltpu.make_async_copy(spots_in_ref, spots_ref, spots_sem)
    spots_copy.start()
    for i in range(2):
        piece_copy(i).start()
    spots_copy.wait()
    count = spots_ref[slots]
    for i in range(2, pieces):
        @pl.when(i * group < count)
        def _(i=i):
            piece_copy(i).start()

    for total in sums:
        total[...] = jnp.zeros_like(total)
    for i in range(pieces):
        @pl.when((i < 2) | (i * group < count))
        def _(i=i):
            piece_copy(i).wait()

            def add_some(turn, carry):
                for way, total in enumerate(sums):
                    k = turn * ways + way
                    spot = jnp.where(k < count, spots_ref[k], spare)
                    total[spot] += staged[k].astype(jnp.float32)
                return carry

            last = jnp.minimum(count, (i + 1) * group)
            lax.fori_loop(i * group // ways, (last + ways - 1) // ways, add_some, 0)

    for h, half in enumerate(halves):
        across = half.shape[1] // blk
        for r in range(half.shape[0] // blk):
            for at in range(across):
                spot = r * sources + order[h * across + at]
                half[r * blk:(r + 1) * blk, at * blk:(at + 1) * blk] = sum(total[spot] for total in sums).astype(half.dtype)


def merge_tiles(spots, values, order, out_blocks):
    slots, blk, _ = values.shape
    group, ways = 16, 2
    smem = pl.BlockSpec(memory_space=pltpu.SMEM)
    vmem = pl.BlockSpec(memory_space=pltpu.VMEM)
    half = jax.ShapeDtypeStruct((out_blocks * blk, len(order) // 2 * blk), jnp.bfloat16)
    return pl.pallas_call(
        functools.partial(merge_kernel, order, group),
        out_shape=[half, half],
        in_specs=[pl.BlockSpec(memory_space=pl.ANY), pl.BlockSpec(memory_space=pltpu.HBM)],
        out_specs=[vmem, vmem],
        scratch_shapes=[
            pltpu.VMEM(values.shape, values.dtype),
            pltpu.SMEM(spots.shape, spots.dtype),
            pltpu.SemaphoreType.DMA((slots // group,)),
            pltpu.SemaphoreType.DMA,
        ] + [pltpu.VMEM((out_blocks * len(order) + 1, blk, blk), jnp.float32)] * ways,
        compiler_params=pltpu.CompilerParams(vmem_limit_bytes=50 * 1024 * 1024),
        cost_estimate=pl.CostEstimate(flops=slots * blk * blk, bytes_accessed=4 * slots * blk * blk, transcendentals=0),
    )(spots, values)


def product_kernel(scale, place_ref, own_tiles_ref, twin_tiles_ref, near_ref, own_in_ref, twin_in_ref, keep_ref, send_ref, own_ref, twin_ref):
    own = jnp.dot(own_tiles_ref[...], near_ref[...], preferred_element_type=jnp.float32)
    twin = jnp.dot(twin_tiles_ref[...], near_ref[...], preferred_element_type=jnp.float32)
    own_ref[...] = own
    twin_ref[...] = twin.astype(twin_ref.dtype)
    across = (((0,), (0,)), ((), ()))
    terms = lax.dot_general(own_in_ref[...], own.astype(jnp.bfloat16), across, preferred_element_type=jnp.float32)
    terms += lax.dot_general(twin_in_ref[...], twin.astype(jnp.bfloat16), across, preferred_element_type=jnp.float32)
    terms *= scale
    rows = terms.shape[0] // 2
    upper = place_ref[0] == 0
    keep_ref[...] = jnp.where(upper, terms[:rows], terms[rows:])
    send_ref[...] = jnp.where(upper, terms[rows:], terms[:rows]).astype(send_ref.dtype)


def products(place, own_tiles, twin_tiles, near, own_in, twin_in, scale):
    rows, features = own_tiles.shape[0], near.shape[1]
    vmem = pl.BlockSpec(memory_space=pltpu.VMEM)
    part = (own_in.shape[1] // 2, features)
    return pl.pallas_call(
        functools.partial(product_kernel, scale),
        out_shape=[
            jax.ShapeDtypeStruct(part, jnp.float32),
            jax.ShapeDtypeStruct(part, jnp.bfloat16),
            jax.ShapeDtypeStruct((rows, features), jnp.float32),
            jax.ShapeDtypeStruct((rows, features), jnp.bfloat16),
        ],
        in_specs=[pl.BlockSpec(memory_space=pltpu.SMEM)] + [vmem] * 5,
        out_specs=[vmem] * 4,
        compiler_params=pltpu.CompilerParams(vmem_limit_bytes=24 * 1024 * 1024),
        cost_estimate=pl.CostEstimate(flops=4 * own_tiles.size * features, bytes_accessed=4 * own_tiles.size, transcendentals=0),
    )(place, own_tiles, twin_tiles, near, own_in, twin_in)


def core_swap(value, masks, total):
    return lax.ppermute(value, both, [(i, i ^ masks[i % 2]) for i in range(total)])


def quad_sum(value, low, high, total):
    third = core_swap(value, [a | b for a, b in zip(low, high)], total)
    second = core_swap(value, high, total)
    first = core_swap(value, low, total)
    f32 = jnp.float32
    return (third.astype(f32) + second.astype(f32)) + (first.astype(f32) + value.astype(f32))


def pair_body(grad_out, relu_mask, layer_input, weight, tile_values, tile_rows, tile_cols, tile_count):
    rep, row = lax.axis_size("rep"), lax.axis_size("row")
    total = rep * row
    blk = tile_values.shape[1]
    masked = grad_out * relu_mask.astype(jnp.bfloat16)
    rep_id, row_id = lax.axis_index("rep"), lax.axis_index("row")
    core_id = row_id % 2
    place = core_id.astype(jnp.int32).reshape(1)

    top = row // 4
    order = [0, 3 * top, 2 * top, top]
    near = jnp.concatenate([masked] + [swap(masked, m, total) for m in order[1:]], 0)
    spots = (tile_rows ^ rep_id) * row + (tile_cols ^ row_id)
    spots = jnp.concatenate([spots, tile_count])
    order = order + [o + 2 for o in order]
    order = order + [o + 1 for o in order]
    other_in = swap(layer_input, row, total)
    own_tiles, far_tiles = merge_tiles(spots, tile_values, order, rep)
    other_in, own_tiles, far_tiles, near = lax.optimization_barrier((other_in, own_tiles, far_tiles, near))
    near = jnp.concatenate([near, swap(near, 2, total)], 0)
    own_in = jnp.concatenate([layer_input, other_in], 0)
    rows = far_tiles.shape[0] // 2
    twin_tiles = jnp.concatenate([swap(far_tiles[i * rows:(i + 1) * rows], 1, total) for i in range(2)], 0)
    twin_in = swap(own_in, 1, total)
    near, own_in, twin_in, twin_tiles = lax.optimization_barrier((near, own_in, twin_in, twin_tiles))
    keep, send, own, twin = products(place, own_tiles, twin_tiles, near, own_in, twin_in, 1.0 / (blk * total) ** 0.5)

    part = (keep + swap(send, 1, total)).astype(jnp.bfloat16)
    part = lax.optimization_barrier(part)
    part = quad_sum(part, (top, row), (2 * top, top // 2), total).astype(jnp.bfloat16)
    part = lax.optimization_barrier(part)
    part = quad_sum(part, (row, top), (top // 2, 2 * top), total)
    part = lax.optimization_barrier(part)
    other = swap(part, 1, total)
    grad_weight = jnp.where(core_id == 0, jnp.concatenate([part, other], 0), jnp.concatenate([other, part], 0))

    cross = jnp.concatenate([own[blk:].astype(jnp.bfloat16), twin[blk:]], 0)
    cross = swap(cross, row, total).astype(jnp.float32)
    twin = (twin[:blk].astype(jnp.float32) + cross[blk:]).astype(jnp.bfloat16)
    prop = (own[:blk] + cross[:blk] + swap(twin, 1, total).astype(jnp.float32)).astype(jnp.bfloat16)
    grad_input = lax.dot_general(
        prop, weight, (((1,), (1,)), ((), ())), preferred_element_type=jnp.float32
    ).astype(jnp.bfloat16)
    return (grad_input, grad_weight)


def solution(mesh):
    placed = (
        P(both, None),
        P(both, None),
        P(both, None),
        P(),
        P(both, None, None),
        P(both),
        P(both),
        P(both),
    )
    merged = mesh.shape["rep"] == 2 and mesh.shape["row"] == 16
    return jax.shard_map(
        pair_body if merged else general_body,
        mesh=mesh,
        in_specs=placed,
        out_specs=(P(both, None), P()),
        check_vma=False,
    )
```
